128 devices in a mesh: segment: 8 (over z, x_hi), shard: 16 (over y, x_lo, core).
Axes of the slice: x: 4 (x_hi: 2, x_lo: 2; x = x_hi * 2 + x_lo), y: 4, z: 4, core: 2. Of those that a mesh axis runs over, the one named last changes fastest.
Arguments:
- tokens_in: bfloat16 [4, 128, 8192], P(None, 'shard'), may hold values from -20 to 20
- weights: bfloat16 [8, 8192, 8192], P('segment', None, 'shard'), may hold values from -0.0625 to 0.0625
Outputs:
- activations: bfloat16 [8, 4, 128, 8192], P('segment', None, 'shard')
- gram: float32 [8, 8192, 8192], P('segment', 'shard')
The draws below stay inside these ranges and needn't reach their ends.
All inputs are finite; a program needn't handle non-finite values.
Results may differ from the reference program's by a relative error of at most 0.015.
Values may be sent and summed in bfloat16 or wider, within the bound.
No kernel may reach another device: no remote copies, remote signals or barrier semaphores. Data moves between devices by JAX's collectives and lax.ppermute only.
A program may use at most 192 MiB of HBM per device.

```python
import math
import jax
import jax.numpy as jnp
from jax import lax

DW = 8192
MICRO = 4
TOK_MB = 128
SECTIONS = 8


def draw_tokens_in(key, part):
    key = jax.random.fold_in(key, 7)
    value_key, row_key, column_key = jax.random.split(key, 3)
    shape = (MICRO, TOK_MB, DW)
    entries = jnp.clip(jax.random.normal(value_key, shape, jnp.float32), -4.0, 4.0)
    row_scale = jnp.exp(jax.random.uniform(row_key, (MICRO, TOK_MB, 1), jnp.float32, math.log(0.3), math.log(3.0)))
    column_scale = jnp.exp(jax.random.uniform(column_key, (1, 1, DW), jnp.float32, math.log(0.3), math.log(3.0)))
    return (0.5 * entries * row_scale * column_scale).astype(jnp.bfloat16)


def level_of(stream_key, dims, shards, smallest, top_value):
    level = 1.0
    for position, parts in shards:
        steps = jax.random.uniform(jax.random.fold_in(jax.random.fold_in(stream_key, 6), position), (parts,), jnp.float32, smallest / len(shards), top_value / len(shards))
        level = level * jnp.repeat(jnp.exp(steps), dims[position] // parts).reshape((-1,) + (1,) * (len(dims) - 1 - position))
    return level


def bell_draw(key, dims, scale, bound, pieces=(), dtype=jnp.bfloat16):
    level = level_of(key, dims, pieces, -0.22, 0.18) if pieces else 1.0
    result = jax.random.normal(key, dims, jnp.float32) * scale * level
    return jnp.minimum(jnp.maximum(result, -bound), bound).astype(dtype)


def setup_inputs(seed: int = 0) -> dict:
    key_of = jax.random.split(jax.random.key(seed), 3)
    return {
        "tokens_in": draw_tokens_in(jax.random.fold_in(key_of[2], 71), 0),
        "weights": bell_draw(key_of[1], (SECTIONS, DW, DW), DW ** -0.5, 0.0625, ((0, 8), (2, 16))),
    }


epsilon = 1e-05

def reference(tokens_in, weights):
    count = MICRO * TOK_MB
    current = tokens_in
    outputs = []
    grams = []
    for section in range(SECTIONS):
        floats = current.astype(jnp.float32)
        mean_square = lax.optimization_barrier(jnp.mean(floats * floats, axis=-1, keepdims=True))
        normed = (floats * lax.rsqrt(mean_square + epsilon)).astype(jnp.bfloat16)
        flat = normed.reshape(count, DW).astype(jnp.float32)
        product = jnp.dot(flat, weights[section].astype(jnp.float32), precision=lax.Precision.HIGHEST)
        gram_matrix = jnp.dot(flat.T, flat, precision=lax.Precision.HIGHEST) / count
        current = (floats + product.reshape(floats.shape)).astype(jnp.bfloat16)
        outputs.append(current)
        grams.append(gram_matrix)
    return (jnp.stack(outputs), jnp.stack(grams))
```

```python
import jax
import jax.numpy as jnp
from jax import lax
from jax.sharding import PartitionSpec as P

epsilon = 1e-05
AXES = ("segment", "shard")
SEGMENTS, ROWS, COLUMNS, CORES = 8, 4, 2, 2


def shard_of(row, column, core):
    return (row * COLUMNS + column) * CORES + core


def move(value, segments, target):
    pairs = []
    for s in segments:
        for row in range(ROWS):
            for column in range(COLUMNS):
                for core in range(CORES):
                    t, r, c, k = target(s, row, column, core)
                    pairs.append((s * 16 + shard_of(row, column, core), t * 16 + shard_of(r % ROWS, c, k)))
    return lax.ppermute(value, AXES, pairs)


def to_sibling(value, segments):
    return move(value, segments, lambda s, r, c, k: (s, r, c, 1 - k))


def up_rows(value, segments, by):
    return move(value, segments, lambda s, r, c, k: (s, r + by, c, k))


def next_segment(value, segments):
    return move(value, segments, lambda s, r, c, k: (s + 1, r, k, c))


def body(tokens_in, weights):
    micros, rows, features = tokens_in.shape
    shards = 16
    batch = rows * shards
    block = features // 8
    half = block // 2
    device = lax.axis_index("shard")
    segment = lax.axis_index("segment")
    core = device % 2
    column = device // 2 % 2
    row = device // 4
    everyone = range(SEGMENTS)

    pieces = weights[0].reshape(ROWS, COLUMNS, block, half)
    order = [0, 1, 3, 2]

    def rows_of(which):
        parts = [lax.dynamic_slice(pieces, ((row + ROWS - by) % ROWS, which, 0, 0), (1, 1, block, half)) for by in order]
        return jnp.concatenate([p[0, 0] for p in parts], axis=0)

    kept = rows_of(core)
    swapped = to_sibling(rows_of(1 - core), everyone)

    split = tokens_in.reshape(micros, rows, ROWS, COLUMNS, block)
    outgoing = jnp.stack([split[:, :, r, k] for r in range(ROWS) for c in range(COLUMNS) for k in range(CORES)])
    arrived = lax.all_to_all(outgoing, "shard", 0, 0)
    tokens = arrived.transpose(1, 0, 2, 3).reshape(micros, batch, block)

    normed_all = jnp.zeros((micros, batch, features), jnp.bfloat16)
    acts_all = jnp.zeros((micros, batch, half), jnp.bfloat16)
    chip_block = None
    for tick in range(micros + SEGMENTS - 1):
        live = [s for s in everyone if 0 <= tick - s < micros]
        group = tick - segment
        slot = jnp.clip(group, 0, micros - 1)
        if tick == 0:
            held = tokens[0]
        else:
            held = next_segment(chip_block, [s - 1 for s in live if s > 0])
            if tick < micros:
                held = jnp.where(segment == 0, tokens[tick], held)
        gathered = [held] + [up_rows(held, live, by) for by in order[1:]]
        other_held = to_sibling(held, live)
        inputs = jnp.concatenate(gathered, axis=1)
        floats = inputs.astype(jnp.float32)
        squares = jnp.sum(floats * floats, axis=1, keepdims=True)
        mine = jnp.dot(inputs, kept, preferred_element_type=jnp.float32)
        others = jnp.dot(inputs, swapped, preferred_element_type=jnp.float32)
        summary = jnp.broadcast_to(squares, (batch, 128))
        came = to_sibling(jnp.concatenate([mine, others, summary], axis=1), live)
        total = squares + came[:, 2 * half : 2 * half + 1]
        scale = lax.rsqrt(total / features + epsilon)
        mine = mine + came[:, half : 2 * half]
        others = others + came[:, :half]
        product = jnp.where(core == 0, jnp.concatenate([mine, others], 1), jnp.concatenate([others, mine], 1))
        residual = jnp.where(core == column, held, other_held)
        chip_block = (residual.astype(jnp.float32) + product * scale).astype(jnp.bfloat16)
        own = lax.dynamic_slice(chip_block, (0, core * half), (batch, half))
        sibling_rest = to_sibling(inputs[:, block:], live)
        full = jnp.zeros((batch, features), jnp.bfloat16)
        for which, blocks in ((core, gathered), (1 - core, [other_held] + [sibling_rest[:, i * block : (i + 1) * block] for i in range(3)])):
            for by, part in zip(order, blocks):
                place = ((row + ROWS - by) % ROWS * COLUMNS + which) * block
                full = lax.dynamic_update_slice(full, part, (0, place))
        normed = (full.astype(jnp.float32) * scale).astype(jnp.bfloat16)
        if tick >= micros:
            active = group < micros
            normed = jnp.where(active, normed, lax.dynamic_index_in_dim(normed_all, slot, 0, keepdims=False))
            own = jnp.where(active, own, lax.dynamic_index_in_dim(acts_all, slot, 0, keepdims=False))
        normed_all = lax.dynamic_update_index_in_dim(normed_all, normed, slot, 0)
        acts_all = lax.dynamic_update_index_in_dim(acts_all, own, slot, 0)

    outgoing = acts_all.reshape(micros, shards, rows, half).transpose(1, 0, 2, 3)
    arrived = lax.all_to_all(outgoing, "shard", 0, 0)
    outputs = arrived.transpose(1, 2, 0, 3).reshape(micros, rows, features)
    flat = normed_all.reshape(micros * batch, features)
    own_columns = lax.dynamic_slice(flat, (0, device * half), (micros * batch, half))
    gram = lax.dot_general(own_columns, flat, (((0,), (0,)), ((), ())), preferred_element_type=jnp.float32)
    return (outputs[None], (gram / (micros * batch))[None])


def solution(mesh):
    in_specs = (P(None, "shard", None), P("segment", None, "shard"))
    out_specs = (P("segment", None, "shard", None), P("segment", "shard", None))
    return jax.shard_map(body, mesh=mesh, in_specs=in_specs, out_specs=out_specs, check_vma=False)
```

```python
import jax
import jax.numpy as jnp
from jax import lax
from jax.experimental import pallas as pl
from jax.experimental.pallas import tpu as pltpu
from jax.sharding import PartitionSpec as P

epsilon = 1e-05
AXES = ("segment", "shard")
SEGMENTS, ROWS, COLUMNS, CORES = 8, 4, 2, 2
STEPS = (0, 1, 3, 2)
MIB = 1 << 20


def shard_of(row, column, core):
    return (row * COLUMNS + column) * CORES + core


def move(value, target):
    pairs = []
    for s in range(SEGMENTS):
        for row in range(ROWS):
            for column in range(COLUMNS):
                for core in range(CORES):
                    t, r, c, k = target(s, row, column, core)
                    pairs.append((s * 16 + shard_of(row, column, core), t % SEGMENTS * 16 + shard_of(r % ROWS, c, k)))
    return lax.ppermute(value, AXES, pairs)


def to_sibling(value):
    return move(value, lambda s, r, c, k: (s, r, c, 1 - k))


def up_rows(value, by):
    return move(value, lambda s, r, c, k: (s, r + by, c, k))


def next_segment(value):
    return move(value, lambda s, r, c, k: (s + 1, r, k, c))


def whole(shape):
    return pl.BlockSpec(shape, lambda *_: (0,) * len(shape))


def project_kernel(a0, a1, a2, a3, kept, swapped, out):
    step = pl.program_id(0)
    half = kept.shape[1]
    for which, block in enumerate((a0, a1, a2, a3)):

        @pl.when(step == which)
        def _():
            x = block[...]
            floats = x.astype(jnp.float32)
            squares = jnp.sum(floats * floats, axis=1, keepdims=True)
            squares = jnp.broadcast_to(squares, (x.shape[0], 128))
            mine = jnp.dot(x, kept[...], preferred_element_type=jnp.float32)
            others = jnp.dot(x, swapped[...], preferred_element_type=jnp.float32)
            if which == 0:
                out[:, :half] = mine
                out[:, half : 2 * half] = others
                out[:, 2 * half :] = squares
            else:
                out[:, :half] += mine
                out[:, half : 2 * half] += others
                out[:, 2 * half :] += squares


def project(blocks, kept, swapped):
    tokens, block = blocks[0].shape
    half = kept.shape[1]
    return pl.pallas_call(
        project_kernel,
        grid=(len(blocks),),
        in_specs=[whole((tokens, block))] * 4 + [pl.BlockSpec((block, half), lambda i: (i, 0))] * 2,
        out_specs=whole((tokens, 2 * half + 128)),
        out_shape=jax.ShapeDtypeStruct((tokens, 2 * half + 128), jnp.float32),
        compiler_params=pltpu.CompilerParams(vmem_limit_bytes=24 * MIB),
        cost_estimate=pl.CostEstimate(flops=2 * tokens * 8 * half * 2 * half, bytes_accessed=9 * MIB, transcendentals=0),
        name="project",
    )(*blocks, kept, swapped)


def combine(place, own, came, held, other_held, fresh, features):
    tokens, block = held.shape

    def kernel(place, own, came, held, other_held, fresh, block_out, act_out, scale_out):
        half = block // 2
        core, column, segment = place[0], place[1], place[2]
        total = own[:, block:] + came[:, block:]
        scale = lax.rsqrt(total * (1.0 / features) + epsilon)
        scale_out[...] = scale
        factor = scale[:, :1]
        mine = (own[:, :half] + came[:, half:block]) * factor
        others = (own[:, half:block] + came[:, :half]) * factor
        residual = jnp.where(core == column, held[...], other_held[...]).astype(jnp.float32)
        low = (residual[:, :half] + jnp.where(core == 0, mine, others)).astype(jnp.bfloat16)
        high = (residual[:, half:] + jnp.where(core == 0, others, mine)).astype(jnp.bfloat16)
        act_out[...] = jnp.where(core == 0, low, high)
        if fresh is not None:
            last = segment == SEGMENTS - 1
            low = jnp.where(last, fresh[:, :half], low)
            high = jnp.where(last, fresh[:, half:], high)
        block_out[:, :half] = low
        block_out[:, half:] = high

    operands = [own, came, held, other_held]
    if fresh is not None:
        operands.append(fresh)
        run = kernel
    else:
        run = lambda p, a, b, c, d, *outs: kernel(p, a, b, c, d, None, *outs)
    return pl.pallas_call(
        run,
        in_specs=[pl.BlockSpec(memory_space=pltpu.SMEM)] + [pl.BlockSpec(memory_space=pltpu.VMEM)] * len(operands),
        out_specs=[pl.BlockSpec(memory_space=pltpu.VMEM)] * 3,
        out_shape=[
            jax.ShapeDtypeStruct((tokens, block), jnp.bfloat16),
            jax.ShapeDtypeStruct((tokens, block // 2), jnp.bfloat16),
            jax.ShapeDtypeStruct((tokens, 128), jnp.float32),
        ],
        compiler_params=pltpu.CompilerParams(vmem_limit_bytes=24 * MIB),
        cost_estimate=pl.CostEstimate(flops=8 * tokens * block, bytes_accessed=2 * MIB, transcendentals=0),
        name="combine",
    )(place, *operands)


def record(table, blocks, others, rest, scale, act, slots, features, kept_so_far):
    tokens, block = blocks[0].shape

    def kernel(table, a0, a1, a2, a3, b0, rest, scale, act, *refs):
        normed_out, acts_out = refs[-2:]
        step = pl.program_id(0)
        factor = scale[:, :1]
        for which, value in enumerate((a0, a1, a2, a3, b0)):

            @pl.when(step == which)
            def _():
                normed_out[0] = (value[...].astype(jnp.float32) * factor).astype(jnp.bfloat16)

        for which in range(3):

            @pl.when(step == 5 + which)
            def _():
                part = rest[:, which * block : (which + 1) * block]
                normed_out[0] = (part.astype(jnp.float32) * factor).astype(jnp.bfloat16)

        acts_out[0] = act[...]

    return pl.pallas_call(
        kernel,
        grid_spec=pltpu.PrefetchScalarGridSpec(
            num_scalar_prefetch=1,
            grid=(8,),
            in_specs=[whole((tokens, block))] * 5
            + [whole(rest.shape), whole(scale.shape), whole(act.shape)]
            + [pl.BlockSpec(memory_space=pl.ANY)] * len(kept_so_far),
            out_specs=[
                pl.BlockSpec((1, tokens, block), lambda i, t: (t[0], 0, t[1 + i])),
                pl.BlockSpec((1, tokens, block // 2), lambda i, t: (t[0], 0, 0)),
            ],
        ),
        out_shape=[
            jax.ShapeDtypeStruct((slots, tokens, features), jnp.bfloat16),
            jax.ShapeDtypeStruct((slots, tokens, block // 2), jnp.bfloat16),
        ],
        input_output_aliases={9: 0, 10: 1} if kept_so_far else {},
        compiler_params=pltpu.CompilerParams(vmem_limit_bytes=24 * MIB),
        cost_estimate=pl.CostEstimate(flops=2 * tokens * features, bytes_accessed=5 * MIB, transcendentals=0),
        name="record",
    )(table, *blocks, others, rest, scale, act, *kept_so_far)


def gram_of(device, flat, count, width):
    features = flat.shape[1]
    step = 1024

    def kernel(which, own, columns, out, turned):
        @pl.when(pl.program_id(0) == 0)
        def _():
            turned[...] = own[...].T

        out[...] = jnp.dot(turned[...], columns[...], preferred_element_type=jnp.float32) * (1.0 / count)

    return pl.pallas_call(
        kernel,
        grid_spec=pltpu.PrefetchScalarGridSpec(
            num_scalar_prefetch=1,
            grid=(features // step,),
            in_specs=[
                pl.BlockSpec((count, width), lambda i, d: (0, d[0])),
                pl.BlockSpec((count, step), lambda i, d: (0, i)),
            ],
            out_specs=pl.BlockSpec((width, step), lambda i, d: (0, i)),
            scratch_shapes=[pltpu.VMEM((width, count), flat.dtype)],
        ),
        out_shape=jax.ShapeDtypeStruct((width, features), jnp.float32),
        compiler_params=pltpu.CompilerParams(vmem_limit_bytes=32 * MIB),
        cost_estimate=pl.CostEstimate(flops=2 * count * width * features, bytes_accessed=26 * MIB, transcendentals=0),
        name="gram",
    )(device, flat, flat)


def body(tokens_in, weights):
    micros, rows, features = tokens_in.shape
    shards = 16
    batch = rows * shards
    block = features // 8
    half = block // 2
    device = lax.axis_index("shard")
    segment = lax.axis_index("segment")
    core = device % 2
    column = device // 2 % 2
    row = device // 4
    place = jnp.stack([core, column, segment]).astype(jnp.int32)

    pieces = weights[0].reshape(ROWS, COLUMNS, block, half)

    def rows_of(which):
        parts = [lax.dynamic_slice(pieces, ((row + ROWS - by) % ROWS, which, 0, 0), (1, 1, block, half)) for by in STEPS]
        return jnp.concatenate([p[0, 0] for p in parts], axis=0)

    swapped = to_sibling(rows_of(1 - core))
    kept = rows_of(core)

    split = tokens_in.reshape(micros, rows, ROWS, COLUMNS, block)
    outgoing = jnp.stack(
        [
            jnp.concatenate([split[:1, :, r, k], split[1:, :, r, c]], axis=0)
            for r in range(ROWS)
            for c in range(COLUMNS)
            for k in range(CORES)
        ]
    )
    arrived = lax.all_to_all(outgoing, "shard", 0, 0)
    tokens = arrived.transpose(1, 0, 2, 3).reshape(micros, batch, block)

    stores = ()
    order = [(row + ROWS - by) % ROWS * COLUMNS for by in STEPS]
    order = [o + core for o in order] + [o + 1 - core for o in order]
    held = tokens[0]
    for tick in range(micros + SEGMENTS - 1):
        if tick > 0:
            held = next_segment(chip_block)
        blocks = [held] + [up_rows(held, by) for by in STEPS[1:]]
        other_held = to_sibling(held)
        own = project(blocks, kept, swapped)
        came = to_sibling(own)
        fresh = tokens[tick + 1] if tick + 1 < micros else None
        chip_block, act, scale = combine(place, own, came, held, other_held, fresh, features)
        rest = to_sibling(jnp.concatenate(blocks[1:], axis=1))
        group = tick - segment
        slot = jnp.where((group >= 0) & (group < micros), group, micros)
        table = jnp.stack([slot] + order).astype(jnp.int32)
        stores = record(table, blocks, other_held, rest, scale, act, micros + 1, features, stores)
    normed_all, acts_all = stores

    outgoing = acts_all[:micros].reshape(micros, shards, rows, half).transpose(1, 0, 2, 3)
    arrived = lax.all_to_all(outgoing, "shard", 0, 0)
    outputs = arrived.transpose(1, 2, 0, 3).reshape(micros, rows, features)
    flat = normed_all.reshape((micros + 1) * batch, features)
    gram = gram_of(device.reshape(1).astype(jnp.int32), flat, micros * batch, half)
    return (outputs[None], gram[None])


def solution(mesh):
    in_specs = (P(None, "shard", None), P("segment", None, "shard"))
    out_specs = (P("segment", None, "shard", None), P("segment", "shard", None))
    return jax.shard_map(body, mesh=mesh, in_specs=in_specs, out_specs=out_specs, check_vma=False)
```

```python
import jax
import jax.numpy as jnp
from jax import lax
from jax.experimental import pallas as pl
from jax.experimental.pallas import tpu as pltpu
from jax.sharding import PartitionSpec as P

epsilon = 1e-05
AXES = ("segment", "shard")
SEGMENTS, ROWS, COLUMNS, CORES = 8, 4, 2, 2
STEPS = (0, 1, 3, 2)
MIB = 1 << 20
PARTS = 1


def shard_of(row, column, core):
    return (row * COLUMNS + column) * CORES + core


def move(value, target):
    pairs = []
    for s in range(SEGMENTS):
        for row in range(ROWS):
            for column in range(COLUMNS):
                for core in range(CORES):
                    t, r, c, k = target(s, row, column, core)
                    pairs.append((s * 16 + shard_of(row, column, core), t % SEGMENTS * 16 + shard_of(r % ROWS, c, k)))
    return lax.ppermute(value, AXES, pairs)


def to_sibling(value):
    return move(value, lambda s, r, c, k: (s, r, c, 1 - k))


def up_rows(value, by):
    return move(value, lambda s, r, c, k: (s, r + by, c, k))


def next_segment(value):
    return move(value, lambda s, r, c, k: (s + 1, r, k, c))


def whole(shape):
    return pl.BlockSpec(shape, lambda *_: (0,) * len(shape))


def arrange_weights(place, weights, own):
    features, half = weights.shape
    block = features // (ROWS * COLUMNS)

    def kernel(place, source, out, sems):
        which = place[0] if own else 1 - place[0]
        copies = []
        for i, by in enumerate(STEPS):
            at = lax.rem(place[4] + ROWS - by, ROWS) * COLUMNS + which
            start = pl.multiple_of(at * block, block)
            copies.append(pltpu.make_async_copy(source.at[pl.ds(start, block)], out.at[pl.ds(i * block, block)], sems.at[i]))
        for c in copies:
            c.start()
        for c in copies:
            c.wait()

    return pl.pallas_call(
        kernel,
        in_specs=[pl.BlockSpec(memory_space=pltpu.SMEM), pl.BlockSpec(memory_space=pl.ANY)],
        out_specs=pl.BlockSpec(memory_space=pltpu.VMEM if own else pl.ANY),
        out_shape=(pltpu.VMEM if own else pltpu.HBM)((ROWS * block, half), weights.dtype),
        scratch_shapes=[pltpu.SemaphoreType.DMA((ROWS,))],
        compiler_params=pltpu.CompilerParams(vmem_limit_bytes=8 * MIB),
        cost_estimate=pl.CostEstimate(flops=0, bytes_accessed=8 * MIB, transcendentals=0),
        name="kept_rows" if own else "given_rows",
    )(place, weights)


def near(value):
    def kernel(source, out, sem):
        copy = pltpu.make_async_copy(source, out, sem)
        copy.start()
        copy.wait()

    return pl.pallas_call(
        kernel,
        in_specs=[pl.BlockSpec(memory_space=pl.ANY)],
        out_specs=pl.BlockSpec(memory_space=pltpu.VMEM),
        out_shape=pltpu.VMEM(value.shape, value.dtype),
        scratch_shapes=[pltpu.SemaphoreType.DMA],
        compiler_params=pltpu.CompilerParams(vmem_limit_bytes=8 * MIB),
        cost_estimate=pl.CostEstimate(flops=0, bytes_accessed=8 * MIB, transcendentals=0),
        name="near",
    )(value)


def project(blocks, kept, swapped, after):
    tokens, block = blocks[0].shape
    half = kept.shape[1]

    def kernel(a0, a1, a2, a3, kept, swapped, *refs):
        out = refs[-1]
        step = pl.program_id(0)
        for which, value in enumerate((a0, a1, a2, a3)):

            @pl.when(step == which)
            def _():
                x = value[...]
                floats = x.astype(jnp.float32)
                squares = jnp.sum(floats * floats, axis=1, keepdims=True)
                squares = jnp.broadcast_to(squares, (tokens, 128))
                mine = jnp.dot(x, kept[...], preferred_element_type=jnp.float32)
                others = jnp.dot(x, swapped[...], preferred_element_type=jnp.float32)
                if which == 0:
                    out[:, :half] = mine
                    out[:, half : 2 * half] = others
                    out[:, 2 * half :] = squares
                else:
                    out[:, :half] += mine
                    out[:, half : 2 * half] += others
                    out[:, 2 * half :] += squares

    return pl.pallas_call(
        kernel,
        grid=(len(blocks),),
        in_specs=[whole((tokens, block))] * 4
        + [pl.BlockSpec((block, half), lambda i: (i, 0))] * 2
        + [pl.BlockSpec(memory_space=pl.ANY)] * len(after),
        out_specs=whole((tokens, 2 * half + 128)),
        out_shape=jax.ShapeDtypeStruct((tokens, 2 * half + 128), jnp.float32),
        compiler_params=pltpu.CompilerParams(vmem_limit_bytes=16 * MIB),
        cost_estimate=pl.CostEstimate(flops=2 * tokens * 8 * half * 2 * half, bytes_accessed=9 * MIB, transcendentals=0),
        name="project",
    )(*blocks, kept, swapped, *after)


def combine(place, own, came, held, other_held, fresh, features):
    tokens, block = held.shape

    def kernel(place, own, came, held, other_held, fresh, block_out, scale_out):
        half = block // 2
        core, column, segment = place[0], place[1], place[2]
        total = own[:, block:] + came[:, block:]
        scale = lax.rsqrt(total * (1.0 / features) + epsilon)
        scale_out[...] = scale
        factor = scale[:, :1]
        mine = (own[:, :half] + came[:, half:block]) * factor
        others = (own[:, half:block] + came[:, :half]) * factor
        residual = jnp.where(core == column, held[...], other_held[...]).astype(jnp.float32)
        low = (residual[:, :half] + jnp.where(core == 0, mine, others)).astype(jnp.bfloat16)
        high = (residual[:, half:] + jnp.where(core == 0, others, mine)).astype(jnp.bfloat16)
        if fresh is not None:
            last = segment == SEGMENTS - 1
            low = jnp.where(last, fresh[:, :half], low)
            high = jnp.where(last, fresh[:, half:], high)
        block_out[:, :half] = low
        block_out[:, half:] = high

    operands = [own, came, held, other_held]
    if fresh is not None:
        operands.append(fresh)
        run = kernel
    else:
        run = lambda p, a, b, c, d, *outs: kernel(p, a, b, c, d, None, *outs)
    return pl.pallas_call(
        run,
        in_specs=[pl.BlockSpec(memory_space=pltpu.SMEM)] + [pl.BlockSpec(memory_space=pltpu.VMEM)] * len(operands),
        out_specs=[pl.BlockSpec(memory_space=pltpu.VMEM)] * 2,
        out_shape=[
            jax.ShapeDtypeStruct((tokens, block), jnp.bfloat16),
            jax.ShapeDtypeStruct((tokens, 128), jnp.float32),
        ],
        compiler_params=pltpu.CompilerParams(vmem_limit_bytes=8 * MIB),
        cost_estimate=pl.CostEstimate(flops=8 * tokens * block, bytes_accessed=2 * MIB, transcendentals=0),
        name="combine",
    )(place, *operands)


def record(table, blocks, others, rest, scale, result):
    tokens, block = blocks[0].shape

    def kernel(table, a0, a1, a2, a3, b0, rest, scale, result, out, act, done):
        step = pl.program_id(0)
        act[...] = result[...]
        factor = scale[:, :1]
        done[...] = jnp.zeros_like(done)
        for which, value in enumerate((a0, a1, a2, a3, b0)):

            @pl.when(step == which)
            def _():
                out[...] = (value[...].astype(jnp.float32) * factor).astype(jnp.bfloat16)

        for which in range(3):

            @pl.when(step == 5 + which)
            def _():
                piece = rest[:, which * block : (which + 1) * block]
                out[...] = (piece.astype(jnp.float32) * factor).astype(jnp.bfloat16)

    return pl.pallas_call(
        kernel,
        grid_spec=pltpu.PrefetchScalarGridSpec(
            num_scalar_prefetch=1,
            grid=(8,),
            in_specs=[whole((tokens, block))] * 5
            + [whole(rest.shape), whole(scale.shape), pl.BlockSpec((tokens, block // 2), lambda i, t: (0, t[8]))],
            out_specs=[
                pl.BlockSpec((tokens, block), lambda i, t: (0, t[i])),
                whole((tokens, block // 2)),
                whole((8, 128)),
            ],
        ),
        out_shape=[
            pltpu.HBM((tokens, 8 * block), jnp.bfloat16),
            pltpu.HBM((tokens, block // 2), jnp.bfloat16),
            jax.ShapeDtypeStruct((8, 128), jnp.float32),
        ],
        compiler_params=pltpu.CompilerParams(vmem_limit_bytes=8 * MIB),
        cost_estimate=pl.CostEstimate(flops=16 * tokens * block, bytes_accessed=5 * MIB, transcendentals=0),
        name="record",
    )(table, *blocks, others, rest, scale, result)


def gram_of(place, pieces, micros, width):
    tokens, features = pieces[0][0].shape
    parts = len(pieces[0])
    pieces = [pltpu.with_memory_space_constraint(p, pltpu.HBM) for tick in pieces for p in tick]
    groups = micros * parts
    count = groups * tokens
    step = 1024
    steps = features // step

    def kernel(place, *refs):
        sources, (out, every, own, turned, arrived, own_arrived) = refs[: len(pieces)], refs[len(pieces) :]
        segment, device = place[2], place[3]
        now = pl.program_id(0)
        own_start = pl.multiple_of(device * width, width)

        def copies(s, columns):
            for g in range(groups):
                source = sources[s * parts + g]
                rows = pl.ds(g * tokens, tokens)
                if columns is None:
                    yield pltpu.make_async_copy(source.at[:, pl.ds(own_start, width)], own.at[rows], own_arrived.at[g])
                else:
                    at = pl.ds(columns * step, step)
                    yield pltpu.make_async_copy(source.at[:, at], every.at[columns, rows], arrived.at[columns, g])

        @pl.when(now == 0)
        def _():
            for s in range(SEGMENTS):

                @pl.when(segment == s)
                def _():
                    for columns in [None, *range(steps)]:
                        for c in copies(s, columns):
                            c.start()

            for c in copies(0, None):
                c.wait()
            turned[...] = own[...].T

        for columns in range(steps):

            @pl.when(now == columns)
            def _():
                for c in copies(0, columns):
                    c.wait()
                out[...] = jnp.dot(turned[...], every[columns], preferred_element_type=jnp.float32) * (1.0 / count)

    return pl.pallas_call(
        kernel,
        grid=(steps,),
        in_specs=[pl.BlockSpec(memory_space=pltpu.SMEM)] + [pl.BlockSpec(memory_space=pltpu.HBM)] * len(pieces),
        out_specs=pl.BlockSpec((width, step), lambda i: (0, i)),
        out_shape=jax.ShapeDtypeStruct((width, features), jnp.float32),
        scratch_shapes=[
            pltpu.VMEM((steps, count, step), jnp.bfloat16),
            pltpu.VMEM((count, width), jnp.bfloat16),
            pltpu.VMEM((width, count), jnp.bfloat16),
            pltpu.SemaphoreType.DMA((steps, groups)),
            pltpu.SemaphoreType.DMA((groups,)),
        ],
        compiler_params=pltpu.CompilerParams(vmem_limit_bytes=24 * MIB),
        cost_estimate=pl.CostEstimate(flops=2 * count * width * features, bytes_accessed=26 * MIB, transcendentals=0),
        name="gram",
    )(place, *pieces)


def body(tokens_in, weights):
    micros, rows, features = tokens_in.shape
    shards = 16
    batch = rows * shards
    block = features // 8
    half = block // 2
    device = lax.axis_index("shard")
    segment = lax.axis_index("segment")
    core = device % 2
    column = device // 2 % 2
    row = device // 4
    place = jnp.stack([core, column, segment, device, row]).astype(jnp.int32)

    swapped = near(to_sibling(arrange_weights(place, weights[0], False)))
    kept = arrange_weights(place, weights[0], True)

    split = tokens_in[0].reshape(rows, ROWS, CORES, block).transpose(2, 0, 1, 3).reshape(1, CORES, rows, ROWS * block)
    split = jnp.broadcast_to(split, (ROWS * COLUMNS, CORES, rows, ROWS * block)).reshape(shards, rows, ROWS * block)
    later = tokens_in[1:].reshape(micros - 1, rows, shards, half).transpose(2, 1, 0, 3).reshape(shards, rows, -1)
    arrived = lax.all_to_all(jnp.concatenate([split, later], axis=2), "shard", 0, 0).reshape(batch, -1)
    waiting = arrived[:, ROWS * block :]
    paired = to_sibling(waiting)
    from_rows = [(row + ROWS - by) % ROWS for by in STEPS]
    feature_table = [r * COLUMNS + k for k in (core, 1 - core) for r in from_rows]
    feature_table = jnp.stack(feature_table + [core]).astype(jnp.int32)
    first_blocks = [lax.dynamic_slice(arrived, (0, r * block), (batch, block)) for r in from_rows]

    def fresh_of(micro, lo, hi):
        a, b = (v[lo:hi, (micro - 1) * half : micro * half] for v in (waiting, paired))
        return jnp.where(core == 0, jnp.concatenate([a, b], 1), jnp.concatenate([b, a], 1))

    size = batch // PARTS
    chip_blocks = [None] * PARTS
    after = [()] * PARTS
    inputs, acts = [], []
    for tick in range(micros + SEGMENTS - 1):
        inputs.append([])
        acts.append([])
        for part in range(PARTS):
            lo, hi = part * size, (part + 1) * size
            if tick == 0:
                blocks = [b[lo:hi] for b in first_blocks]
                held = blocks[0]
            else:
                held = next_segment(chip_blocks[part])
                blocks = [held] + [up_rows(held, by) for by in STEPS[1:]]
            other_held = to_sibling(held)
            own = project(blocks, kept, swapped, after[part])
            came = to_sibling(own)
            fresh = fresh_of(tick + 1, lo, hi) if tick + 1 < micros else None
            chip_blocks[part], scale = combine(place, own, came, held, other_held, fresh, features)
            rest = to_sibling(jnp.concatenate(blocks[1:], axis=1))
            normed, act, done = record(feature_table, blocks, other_held, rest, scale, chip_blocks[part])
            inputs[-1].append(normed)
            acts[-1].append(act)
            after[part] = (done,)

    acts = jnp.stack([jnp.concatenate(a, axis=0) for a in acts])
    acts = lax.dynamic_slice(acts, (segment, 0, 0), (micros, batch, half))
    outgoing = acts.reshape(micros, shards, rows, half).transpose(1, 0, 2, 3)
    arrived = lax.all_to_all(outgoing, "shard", 0, 0)
    outputs = arrived.transpose(1, 2, 0, 3).reshape(micros, rows, features)
    return (outputs[None], gram_of(place, inputs, micros, half)[None])


def solution(mesh):
    in_specs = (P(None, "shard", None), P("segment", None, "shard"))
    out_specs = (P("segment", None, "shard", None), P("segment", "shard", None))
    return jax.shard_map(body, mesh=mesh, in_specs=in_specs, out_specs=out_specs, check_vma=False)
```

```python
import jax
import jax.numpy as jnp
from jax import lax
from jax.experimental import pallas as pl
from jax.experimental.pallas import tpu as pltpu
from jax.sharding import PartitionSpec as P

epsilon = 1e-05
AXES = ("segment", "shard")
SEGMENTS, ROWS, COLUMNS, CORES = 8, 4, 2, 2
STEPS = (0, 1, 3, 2)
MIB = 1 << 20
PARTS = 2


def shard_of(row, column, core):
    return (row * COLUMNS + column) * CORES + core


def move(value, target):
    pairs = []
    for s in range(SEGMENTS):
        for row in range(ROWS):
            for column in range(COLUMNS):
                for core in range(CORES):
                    t, r, c, k = target(s, row, column, core)
                    pairs.append((s * 16 + shard_of(row, column, core), t % SEGMENTS * 16 + shard_of(r % ROWS, c, k)))
    return lax.ppermute(value, AXES, pairs)


def to_sibling(value):
    return move(value, lambda s, r, c, k: (s, r, c, 1 - k))


def up_rows(value, by):
    return move(value, lambda s, r, c, k: (s, r + by, c, k))


def next_segment(value):
    return move(value, lambda s, r, c, k: (s + 1, r, k, c))


def whole(shape):
    return pl.BlockSpec(shape, lambda *_: (0,) * len(shape))


def arrange_weights(place, weights, own):
    features, half = weights.shape
    block = features // (ROWS * COLUMNS)

    def kernel(place, source, out, sems):
        which = place[0] if own else 1 - place[0]
        copies = []
        for i, by in enumerate(STEPS):
            at = lax.rem(place[4] + ROWS - by, ROWS) * COLUMNS + which
            start = pl.multiple_of(at * block, block)
            copies.append(pltpu.make_async_copy(source.at[pl.ds(start, block)], out.at[pl.ds(i * block, block)], sems.at[i]))
        for c in copies:
            c.start()
        for c in copies:
            c.wait()

    return pl.pallas_call(
        kernel,
        in_specs=[pl.BlockSpec(memory_space=pltpu.SMEM), pl.BlockSpec(memory_space=pl.ANY)],
        out_specs=pl.BlockSpec(memory_space=pltpu.VMEM),
        out_shape=pltpu.VMEM((ROWS * block, half), weights.dtype),
        scratch_shapes=[pltpu.SemaphoreType.DMA((ROWS,))],
        compiler_params=pltpu.CompilerParams(vmem_limit_bytes=8 * MIB),
        cost_estimate=pl.CostEstimate(flops=0, bytes_accessed=8 * MIB, transcendentals=0),
        name="kept_rows" if own else "given_rows",
    )(place, weights)


def near(value):
    def kernel(source, out, sem):
        copy = pltpu.make_async_copy(source, out, sem)
        copy.start()
        copy.wait()

    return pl.pallas_call(
        kernel,
        in_specs=[pl.BlockSpec(memory_space=pl.ANY)],
        out_specs=pl.BlockSpec(memory_space=pltpu.VMEM),
        out_shape=pltpu.VMEM(value.shape, value.dtype),
        scratch_shapes=[pltpu.SemaphoreType.DMA],
        compiler_params=pltpu.CompilerParams(vmem_limit_bytes=8 * MIB),
        cost_estimate=pl.CostEstimate(flops=0, bytes_accessed=8 * MIB, transcendentals=0),
        name="near",
    )(value)


def project(blocks, kept, swapped, after):
    tokens, block = blocks[0].shape
    half = kept.shape[1]

    def kernel(a0, a1, a2, a3, kept, swapped, *refs):
        out = refs[-1]
        step = pl.program_id(0)
        for which, value in enumerate((a0, a1, a2, a3)):

            @pl.when(step == which)
            def _():
                x = value[...]
                floats = x.astype(jnp.float32)
                squares = jnp.sum(floats * floats, axis=1, keepdims=True)
                squares = jnp.broadcast_to(squares, (tokens, 128))
                mine = jnp.dot(x, kept[...], preferred_element_type=jnp.float32)
                others = jnp.dot(x, swapped[...], preferred_element_type=jnp.float32)
                if which == 0:
                    out[:, :half] = mine
                    out[:, half : 2 * half] = others
                    out[:, 2 * half :] = squares
                else:
                    out[:, :half] += mine
                    out[:, half : 2 * half] += others
                    out[:, 2 * half :] += squares

    return pl.pallas_call(
        kernel,
        grid=(len(blocks),),
        in_specs=[whole((tokens, block))] * 4
        + [pl.BlockSpec((block, half), lambda i: (i, 0))] * 2
        + [pl.BlockSpec(memory_space=pl.ANY)] * len(after),
        out_specs=whole((tokens, 2 * half + 128)),
        out_shape=jax.ShapeDtypeStruct((tokens, 2 * half + 128), jnp.float32),
        compiler_params=pltpu.CompilerParams(vmem_limit_bytes=16 * MIB),
        cost_estimate=pl.CostEstimate(flops=2 * tokens * 8 * half * 2 * half, bytes_accessed=9 * MIB, transcendentals=0),
        name="project",
    )(*blocks, kept, swapped, *after)


def combine(place, own, came, held, other_held, fresh, features):
    tokens, block = held.shape

    def kernel(place, own, came, held, other_held, fresh, block_out, scale_out):
        half = block // 2
        core, column, segment = place[0], place[1], place[2]
        total = own[:, block:] + came[:, block:]
        scale = lax.rsqrt(total * (1.0 / features) + epsilon)
        scale_out[...] = scale
        factor = scale[:, :1]
        mine = (own[:, :half] + came[:, half:block]) * factor
        others = (own[:, half:block] + came[:, :half]) * factor
        residual = jnp.where(core == column, held[...], other_held[...]).astype(jnp.float32)
        low = (residual[:, :half] + jnp.where(core == 0, mine, others)).astype(jnp.bfloat16)
        high = (residual[:, half:] + jnp.where(core == 0, others, mine)).astype(jnp.bfloat16)
        if fresh is not None:
            last = segment == SEGMENTS - 1
            low = jnp.where(last, fresh[:, :half], low)
            high = jnp.where(last, fresh[:, half:], high)
        block_out[:, :half] = low
        block_out[:, half:] = high

    operands = [own, came, held, other_held]
    if fresh is not None:
        operands.append(fresh)
        run = kernel
    else:
        run = lambda p, a, b, c, d, *outs: kernel(p, a, b, c, d, None, *outs)
    return pl.pallas_call(
        run,
        in_specs=[pl.BlockSpec(memory_space=pltpu.SMEM)] + [pl.BlockSpec(memory_space=pltpu.VMEM)] * len(operands),
        out_specs=[pl.BlockSpec(memory_space=pltpu.VMEM)] * 2,
        out_shape=[
            jax.ShapeDtypeStruct((tokens, block), jnp.bfloat16),
            jax.ShapeDtypeStruct((tokens, 128), jnp.float32),
        ],
        compiler_params=pltpu.CompilerParams(vmem_limit_bytes=8 * MIB),
        cost_estimate=pl.CostEstimate(flops=8 * tokens * block, bytes_accessed=2 * MIB, transcendentals=0),
        name="combine",
    )(place, *operands)


def record(table, parts, late):
    block = parts[0][0].shape[1]
    half = block // 2
    sizes = [p[0].shape[0] for p in parts]
    batch = sum(sizes)
    arity = len(parts[0])

    def kernel(table, *refs):
        out, act, done = refs[-3:]
        done[...] = jnp.zeros_like(done)
        at = 0
        for i, size in enumerate(sizes):
            *blocks, rest, scale, result = refs[i * arity : (i + 1) * arity]
            factor = scale[:, :1]
            for which in range(8):
                value = blocks[which][...] if which < 5 else rest[:, (which - 5) * block : (which - 4) * block]
                place = pl.ds(pl.multiple_of(table[which] * block, block), block)
                out[at : at + size, place] = (value.astype(jnp.float32) * factor).astype(jnp.bfloat16)
            act[at : at + size, :] = jnp.where(table[8] == 0, result[:, :half], result[:, half:])
            at += size

    operands = [x for p in parts for x in p]
    return pl.pallas_call(
        kernel,
        grid_spec=pltpu.PrefetchScalarGridSpec(
            num_scalar_prefetch=1,
            grid=(1,),
            in_specs=[whole(x.shape) for x in operands] + [pl.BlockSpec(memory_space=pl.ANY)] * len(late),
            out_specs=[whole((batch, 8 * block)), whole((batch, half)), whole((8, 128))],
        ),
        out_shape=[
            pltpu.HBM((batch, 8 * block), jnp.bfloat16),
            pltpu.HBM((batch, half), jnp.bfloat16),
            jax.ShapeDtypeStruct((8, 128), jnp.float32),
        ],
        compiler_params=pltpu.CompilerParams(vmem_limit_bytes=12 * MIB),
        cost_estimate=pl.CostEstimate(flops=16 * batch * block, bytes_accessed=5 * MIB, transcendentals=0),
        name="record",
    )(table, *operands, *late)


def gram_of(place, pieces, micros, width):
    tokens, features = pieces[0].shape
    count = micros * tokens
    step = 2048
    pieces = [pltpu.with_memory_space_constraint(p, pltpu.HBM) for p in pieces]

    def kernel(place, *refs):
        sources, (out, every, turned, arrived) = refs[: len(pieces)], refs[len(pieces) :]
        segment, device = place[2], place[3]

        @pl.when(pl.program_id(0) == 0)
        def _():
            for s in range(SEGMENTS):

                @pl.when(segment == s)
                def _():
                    copies = [
                        pltpu.make_async_copy(sources[s + m], every.at[pl.ds(m * tokens, tokens)], arrived.at[m])
                        for m in range(micros)
                    ]
                    for c in copies:
                        c.start()
                    for c in copies:
                        c.wait()

            start = pl.multiple_of(device * width, width)
            turned[...] = every[:, pl.ds(start, width)].T

        column = pl.multiple_of(pl.program_id(0) * step, step)
        out[...] = jnp.dot(turned[...], every[:, pl.ds(column, step)], preferred_element_type=jnp.float32) * (
            1.0 / count
        )

    return pl.pallas_call(
        kernel,
        grid=(features // step,),
        in_specs=[pl.BlockSpec(memory_space=pltpu.SMEM)] + [pl.BlockSpec(memory_space=pltpu.HBM)] * len(pieces),
        out_specs=pl.BlockSpec((width, step), lambda i: (0, i)),
        out_shape=jax.ShapeDtypeStruct((width, features), jnp.float32),
        scratch_shapes=[
            pltpu.VMEM((count, features), jnp.bfloat16),
            pltpu.VMEM((width, count), jnp.bfloat16),
            pltpu.SemaphoreType.DMA((micros,)),
        ],
        compiler_params=pltpu.CompilerParams(vmem_limit_bytes=24 * MIB),
        cost_estimate=pl.CostEstimate(flops=2 * count * width * features, bytes_accessed=26 * MIB, transcendentals=0),
        name="gram",
    )(place, *pieces)


def body(tokens_in, weights):
    micros, rows, features = tokens_in.shape
    shards = 16
    batch = rows * shards
    block = features // 8
    half = block // 2
    device = lax.axis_index("shard")
    segment = lax.axis_index("segment")
    core = device % 2
    column = device // 2 % 2
    row = device // 4
    place = jnp.stack([core, column, segment, device, row]).astype(jnp.int32)

    weights = pltpu.with_memory_space_constraint(weights[0], pltpu.HBM)
    swapped = near(to_sibling(arrange_weights(place, weights, False)))
    kept = arrange_weights(place, weights, True)

    split = tokens_in[0].reshape(rows, ROWS, CORES, block).transpose(2, 0, 1, 3).reshape(1, CORES, rows, ROWS * block)
    split = jnp.broadcast_to(split, (ROWS * COLUMNS, CORES, rows, ROWS * block)).reshape(shards, rows, ROWS * block)
    later = tokens_in[1:].reshape(micros - 1, rows, shards, half).transpose(2, 1, 0, 3).reshape(shards, rows, -1)
    arrived = lax.all_to_all(jnp.concatenate([split, later], axis=2), "shard", 0, 0).reshape(batch, -1)
    waiting = arrived[:, ROWS * block :]
    paired = to_sibling(waiting)
    from_rows = [(row + ROWS - by) % ROWS for by in STEPS]
    feature_table = [r * COLUMNS + k for k in (core, 1 - core) for r in from_rows]
    feature_table = jnp.stack(feature_table + [core]).astype(jnp.int32)
    first_blocks = [lax.dynamic_slice(arrived, (0, r * block), (batch, block)) for r in from_rows]

    def fresh_of(micro, lo, hi):
        a, b = (v[lo:hi, (micro - 1) * half : micro * half] for v in (waiting, paired))
        return jnp.where(core == 0, jnp.concatenate([a, b], 1), jnp.concatenate([b, a], 1))

    size = batch // PARTS
    chip_blocks = [None] * PARTS
    inputs, acts, waiting_parts = [], [], None

    def store(parts, late):
        normed, act, done = record(feature_table, parts, late)
        inputs.append(normed)
        acts.append(act)
        return (done,)

    for tick in range(micros + SEGMENTS - 1):
        if tick == 0:
            helds = [first_blocks[0][p * size : (p + 1) * size] for p in range(PARTS)]
            after = ()
        else:
            helds = [next_segment(c) for c in chip_blocks]
            after = store(waiting_parts, (helds[-1],))
        waiting_parts = []
        for part, held in enumerate(helds):
            lo, hi = part * size, (part + 1) * size
            if tick == 0:
                blocks = [b[lo:hi] for b in first_blocks]
            else:
                blocks = [held] + [up_rows(held, by) for by in STEPS[1:]]
            other_held = to_sibling(held)
            own = project(blocks, kept, swapped, after)
            came = to_sibling(own)
            fresh = fresh_of(tick + 1, lo, hi) if tick + 1 < micros else None
            chip_blocks[part], scale = combine(place, own, came, held, other_held, fresh, features)
            rest = to_sibling(jnp.concatenate(blocks[1:], axis=1))
            waiting_parts.append([*blocks, other_held, rest, scale, chip_blocks[part]])
    store(waiting_parts, ())

    acts = lax.dynamic_slice(jnp.stack(acts), (segment, 0, 0), (micros, batch, half))
    outgoing = acts.reshape(micros, shards, rows, half).transpose(1, 0, 2, 3)
    arrived = lax.all_to_all(outgoing, "shard", 0, 0)
    outputs = arrived.transpose(1, 2, 0, 3).reshape(micros, rows, features)
    return (outputs[None], gram_of(place, inputs, micros, half)[None])


def solution(mesh):
    in_specs = (P(None, "shard", None), P("segment", None, "shard"))
    out_specs = (P("segment", None, "shard", None), P("segment", "shard", None))
    return jax.shard_map(body, mesh=mesh, in_specs=in_specs, out_specs=out_specs, check_vma=False)
```
